32 devices in a mesh: row: 16 (over z, x, core), col: 2 (over y).
Axes of the slice: x: 2, y: 2, z: 4, core: 2. Of those that a mesh axis runs over, the one named last changes fastest.
Arguments:
- object_field: float32 [2, 2, 4096, 512], P(None, None, 'row', 'col'), may hold values from -4 to 4
- probe_wave: float32 [2, 256, 256], replicated, may hold values from -6 to 6
- positions: int32 [16, 2, 6, 2], P('row', 'col'), may hold values from 0 to 256, as said below
- counts: int32 [16, 2], P('row', 'col'), may hold values from 1 to 6, as said below
- amplitudes: bfloat16 [16, 2, 6, 256, 256], P('row', 'col'), may hold values from 0 to 3
Outputs:
- updated_object: float32 [2, 2, 4096, 512], P(None, None, 'row', 'col')
The draws below stay inside these ranges and needn't reach their ends.
Inputs may be any that keep to these rules, and one draw needn't show every extreme that they name: `positions`: the window of a slot covers 256 x 256 pixels of a frame that begins 128 pixels above and left of its tile. Slots at and after the tile's count are unused. `counts`: some tile uses all 6 slots in every draw.
All inputs are finite; a program needn't handle non-finite values.
Results may differ from the reference program's by a relative error of at most 0.024.
Values may be sent and summed in bfloat16 or wider, within the bound.
A program may use at most 64 MiB of HBM per device.

```python
import jax
import jax.numpy as jnp
from jax import lax

PROBE = 256
TILE = 256
P_MAX = 6
ITERS = 2
NY = 4096
NX = 512
N_ROW = 16
N_COL = 2


def draw_positions(key, part):
    subkeys = jax.random.split(jax.random.fold_in(key, 11), 3)
    entries = N_ROW * N_COL * P_MAX * 2
    flattened = jax.random.randint(subkeys[0], (entries,), 0, TILE + 1, dtype=jnp.int32)
    low_at = jax.random.randint(subkeys[1], (), 0, entries, dtype=jnp.int32)
    high_at = (low_at + 1 + jax.random.randint(subkeys[2], (), 0, entries - 1, dtype=jnp.int32)) % entries
    flattened = flattened.at[low_at].set(0).at[high_at].set(TILE)
    return flattened.reshape(N_ROW, N_COL, P_MAX, 2).astype(jnp.int32)


def draw_counts(key, part):
    subkeys = jax.random.split(jax.random.fold_in(key, 23), 3)
    baseline = jax.random.randint(subkeys[0], (N_ROW, N_COL), 1, 3, dtype=jnp.int32)
    crowded = jax.random.randint(subkeys[1], (N_ROW, N_COL), 0, 8, dtype=jnp.int32) == 0
    filled = jnp.where(crowded, P_MAX, baseline)
    chosen = jax.random.randint(subkeys[2], (), 0, N_ROW * N_COL, dtype=jnp.int32)
    flattened = filled.reshape(-1).at[chosen].set(P_MAX)
    return flattened.reshape(N_ROW, N_COL).astype(jnp.int32)


def block_scale(key, shape, cuts, low, largest):
    loudness, own = 1.0, jax.random.fold_in(key, 6)
    for position, parts in cuts:
        draws = jnp.exp(jax.random.uniform(jax.random.fold_in(own, position), (parts,), jnp.float32, low / len(cuts), largest / len(cuts)))
        loudness = loudness * jnp.repeat(draws, shape[position] // parts).reshape([-1 if axis == position else 1 for axis in range(len(shape))])
    return loudness


def bell_draw(stream_key, shape, scale, bound, pieces=(), kind=jnp.bfloat16):
    array = jax.random.normal(stream_key, shape, jnp.float32) * scale
    if len(pieces) > 0:
        array = block_scale(stream_key, shape, pieces, -0.22, 0.18) * array
    return jnp.clip(array, min=-bound, max=bound).astype(kind)


def setup_inputs(seed: int = 0) -> dict:
    seeds = jax.random.split(jax.random.key(seed), 6)
    object_field = bell_draw(seeds[0], (2, 2, NY, NX), 0.5, 4.0, ((2, 16), (3, 2)), jnp.float32)
    probe_wave = bell_draw(seeds[1], (2, PROBE, PROBE), 1.0, 6.0, (), jnp.float32)
    positions = draw_positions(jax.random.fold_in(seeds[5], 71), 0)
    counts = draw_counts(jax.random.fold_in(seeds[5], 71), 0)
    amplitudes = jnp.clip(3.0 * jax.random.uniform(seeds[4], (N_ROW, N_COL, P_MAX, PROBE, PROBE), jnp.float32) ** block_scale(seeds[4], (N_ROW, N_COL, P_MAX, PROBE, PROBE), ((0, 16), (1, 2)), -0.2, 0.2), 0.0, 3.0).astype(jnp.bfloat16)
    return {"object_field": object_field, "probe_wave": probe_wave, "positions": positions, "counts": counts, "amplitudes": amplitudes}


smooth_floor = 0.25
descent_rate = 0.1

def make_tables(points):
    indices = jnp.arange(points, dtype=jnp.int32)
    products = indices[:, None] * indices[None, :] % points
    phases = 2.0 * jnp.pi / points * products.astype(jnp.float32)
    scaling = 1.0 / jnp.sqrt(jnp.float32(points))
    cosines = jnp.cos(phases)
    sine_table = jnp.sin(phases)
    fourier = ((cosines * scaling).astype(jnp.bfloat16), (-sine_table * scaling).astype(jnp.bfloat16))
    frequency = jnp.where(indices < points // 2, indices, indices - points).astype(jnp.float32)
    chirp_phase = -jnp.pi / (2.0 * points) * frequency * frequency
    chirp_cos = jnp.cos(chirp_phase)[None, :]
    chirp_sin = jnp.sin(chirp_phase)[None, :]
    highest = lax.Precision.HIGHEST
    cos_real = jnp.dot(cosines * chirp_cos, cosines, precision=highest)
    sin_real = jnp.dot(sine_table * chirp_cos, sine_table, precision=highest)
    sin_imag = jnp.dot(sine_table * chirp_sin, cosines, precision=highest)
    cos_imag = jnp.dot(cosines * chirp_sin, sine_table, precision=highest)
    mixed_one = jnp.dot(sine_table * chirp_cos, cosines, precision=highest)
    mixed_two = jnp.dot(cosines * chirp_cos, sine_table, precision=highest)
    plain_one = jnp.dot(cosines * chirp_sin, cosines, precision=highest)
    plain_two = jnp.dot(sine_table * chirp_sin, sine_table, precision=highest)
    kernel_real = (cos_real + sin_real - sin_imag + cos_imag) / points
    kernel_imaginary = (mixed_one - mixed_two + plain_one + plain_two) / points
    propagator = (kernel_real.astype(jnp.bfloat16), kernel_imaginary.astype(jnp.bfloat16))
    return (fourier, propagator)

def complex_product(left_factor, right_factor):
    return (left_factor[0] * right_factor[0] - left_factor[1] * right_factor[1], left_factor[0] * right_factor[1] + left_factor[1] * right_factor[0])

def conjugate(operand):
    return (operand[0], -operand[1])

def to_half(operand):
    return (operand[0].astype(jnp.bfloat16), operand[1].astype(jnp.bfloat16))

def apply_left(matrix, operand):
    rows_count = matrix[0].shape[0]
    cols_count = operand[0].shape[1]
    stacked = jnp.concatenate([matrix[0], matrix[1]], axis=0)
    joined = jnp.concatenate([operand[0], operand[1]], axis=1)
    result = jnp.dot(stacked, joined, preferred_element_type=jnp.float32)
    return (result[:rows_count, :cols_count] - result[rows_count:, cols_count:], result[:rows_count, cols_count:] + result[rows_count:, :cols_count])

def apply_right(operand, matrix):
    rows_count = operand[0].shape[0]
    cols_count = matrix[0].shape[1]
    stacked = jnp.concatenate([operand[0], operand[1]], axis=0)
    joined = jnp.concatenate([matrix[0], matrix[1]], axis=1)
    result = jnp.dot(stacked, joined, preferred_element_type=jnp.float32)
    return (result[:rows_count, :cols_count] - result[rows_count:, cols_count:], result[:rows_count, cols_count:] + result[rows_count:, :cols_count])

def transform(matrix, operand):
    return apply_right(to_half(apply_left(matrix, operand)), matrix)

def slot_gradient(window, probe_field, measured, tables):
    fourier, propagator = tables
    layers = window.astype(jnp.float32)
    first_layer = (1.0 + layers[0, 0], layers[0, 1])
    second_layer = (1.0 + layers[1, 0], layers[1, 1])
    entrance = to_half(complex_product(probe_field, first_layer))
    middle = to_half(transform(propagator, entrance))
    middle_wide = (middle[0].astype(jnp.float32), middle[1].astype(jnp.float32))
    leaving = to_half(complex_product(middle_wide, second_layer))
    distant = transform(fourier, leaving)
    modulus = jnp.sqrt(distant[0] * distant[0] + distant[1] * distant[1] + smooth_floor)
    factor = 1.0 - measured.astype(jnp.float32) / modulus
    residual = to_half((factor * distant[0], factor * distant[1]))
    back_far = transform(conjugate(fourier), residual)
    back_middle = to_half(complex_product(back_far, conjugate(second_layer)))
    back_near = transform(conjugate(propagator), back_middle)
    first_grad = complex_product(back_near, conjugate(probe_field))
    second_grad = complex_product(back_far, conjugate(middle_wide))
    return jnp.stack([jnp.stack(first_grad), jnp.stack(second_grad)])

def window_at(source, corner, extent):
    anchor = jnp.zeros((), jnp.int32)
    return lax.dynamic_slice(source, (anchor, anchor, corner[0], corner[1]), (2, 2, extent, extent))

def add_window(accumulated, corner, update):
    extent = update.shape[-1]
    anchor = jnp.zeros((), jnp.int32)
    current = window_at(accumulated, corner, extent)
    return lax.dynamic_update_slice(accumulated, current + update, (anchor, anchor, corner[0], corner[1]))

def reference(object_field, probe_wave, positions, counts, amplitudes):
    probe_size = probe_wave.shape[1]
    half_width = probe_size // 2
    tables = make_tables(probe_size)
    probe_field = (probe_wave[0], probe_wave[1])
    slot_count = N_ROW * N_COL * P_MAX
    corners = positions.reshape(slot_count, 2).astype(jnp.int32)
    measured_all = amplitudes.reshape(slot_count, probe_size, probe_size)
    slot_numbers = jnp.arange(slot_count, dtype=jnp.int32)
    tile_index = slot_numbers // P_MAX
    active_slots = slot_numbers % P_MAX < counts.reshape(-1).astype(jnp.int32)[tile_index]
    offsets = jnp.stack([tile_index // N_COL * TILE, tile_index % N_COL * TILE], axis=1).astype(jnp.int32)
    global_corners = (corners + offsets).astype(jnp.int32)
    current = object_field
    for iteration in range(ITERS):
        padded = jnp.pad(current.astype(jnp.bfloat16), ((0, 0), (0, 0), (half_width, half_width), (half_width, half_width)))

        def compute(window, measured):
            return slot_gradient(window, probe_field, measured, tables)

        def nothing(window, measured):
            return jnp.zeros((2, 2, probe_size, probe_size), jnp.float32)

        def visit_slot(accumulated, element):
            corner, active, measured = element
            window = window_at(padded, corner, probe_size)
            update = lax.cond(active, compute, nothing, window, measured)
            return (add_window(accumulated, corner, update), None)
        gradient = lax.scan(visit_slot, jnp.zeros(padded.shape, jnp.float32), (global_corners, active_slots, measured_all))[0]
        current = current - descent_rate * gradient[:, :, half_width:half_width + NY, half_width:half_width + NX]
    return current
```

```python
import functools

import jax
import jax.numpy as jnp
import ml_dtypes
import numpy as np
from jax import lax
from jax.experimental import pallas as pl
from jax.experimental.pallas import tpu as pltpu
from jax.sharding import PartitionSpec as P

ITERS = 2
LANES = 128
ROWS = 8

smooth_floor = 0.25
descent_rate = 0.1


def passed_along(value, axis, steps):
    count = lax.axis_size(axis)
    leading, last = (max(0, -steps), min(count, count - steps))
    return lax.ppermute(value, axis, [(source, source + steps) for source in range(leading, last)])


def make_tables(points):
    indices = np.arange(points)
    phases = 2.0 * np.pi / points * (indices[:, None] * indices[None, :] % points)
    fourier = np.exp(-1j * phases) / np.sqrt(points)
    frequency = np.where(indices < points // 2, indices, indices - points).astype(np.float64)
    chirp = np.exp(-1j * np.pi / (2.0 * points) * frequency * frequency)
    kernel = (np.exp(1j * phases) @ chirp) / points
    propagator = kernel[(indices[:, None] - indices[None, :]) % points]
    forms = []
    for matrix in (fourier, propagator):
        real = matrix.real.astype(np.float32).astype(ml_dtypes.bfloat16)
        imag = matrix.imag.astype(np.float32).astype(ml_dtypes.bfloat16)
        forms.append(np.block([[real, -imag], [imag, real]]))
        forms.append(np.block([[real, imag], [-imag, real]]))
    return [jnp.asarray(form) for form in forms]


def transform(left_form, right_form, real, imag):
    size = real.shape[0]
    stacked = jnp.concatenate([real.astype(jnp.bfloat16), imag.astype(jnp.bfloat16)], axis=0)
    inner = jnp.dot(left_form[...], stacked, preferred_element_type=jnp.float32)
    inner = inner.astype(jnp.bfloat16)
    joined = jnp.concatenate([inner[:size], inner[size:]], axis=1)
    outer = jnp.dot(joined, right_form[...], preferred_element_type=jnp.float32)
    return outer[:, :size], outer[:, size:]


def rounded(value):
    return value.astype(jnp.bfloat16).astype(jnp.float32)


def slots_kernel(
    corners, used, core, left, right, top, bottom, probe, measured_all,
    fourier_left, fourier_right, near_left, near_right,
    inside, upper_rim, lower_rim, frame, total,
):
    size = probe.shape[1]
    half = size // 2
    tile = core.shape[2]
    full = tile + 2 * half
    wide = size + LANES
    tall = size + ROWS
    for part in range(2):
        lift = 1.0 if part == 0 else 0.0
        for layer in range(2):
            at = (layer, part)
            frame[layer, part, half : half + tile, half : half + tile] = (
                core[at].astype(jnp.bfloat16).astype(jnp.float32) + lift
            )
            frame[layer, part, half : half + tile, :half] = left[at].astype(jnp.float32) + lift
            frame[layer, part, half : half + tile, half + tile : full] = (
                right[at].astype(jnp.float32) + lift
            )
            frame[layer, part, :half, :full] = top[at].astype(jnp.float32) + lift
            frame[layer, part, half + tile : full, :full] = bottom[at].astype(jnp.float32) + lift
    total[...] = jnp.zeros_like(total)

    def one_slot(slot, carry):
        y = corners[slot, 0]
        x = corners[slot, 1]
        shift = lax.rem(x, LANES)
        base = pl.multiple_of(x - shift, LANES)
        down = lax.rem(y, ROWS)
        start = pl.multiple_of(y - down, ROWS)

        def window(layer, part):
            value = frame[layer, part, pl.ds(start, tall), pl.ds(base, wide)]
            value = pltpu.roll(value, lax.rem(wide - shift, wide), 1)[:, :size]
            return pltpu.roll(value, lax.rem(tall - down, tall), 0)[:size]

        def add(layer, part, value):
            value = jnp.concatenate([value, jnp.zeros((ROWS, size), jnp.float32)], axis=0)
            value = pltpu.roll(value, down, 0)
            value = jnp.concatenate([value, jnp.zeros((tall, LANES), jnp.float32)], axis=1)
            total[layer, part, pl.ds(start, tall), pl.ds(base, wide)] += pltpu.roll(value, shift, 1)

        fr, fi = window(0, 0), window(0, 1)
        pr, pi = probe[0], probe[1]
        mr, mi = transform(near_left, near_right, pr * fr - pi * fi, pr * fi + pi * fr)
        mr, mi = rounded(mr), rounded(mi)
        sr, si = window(1, 0), window(1, 1)
        dr, di = transform(fourier_left, fourier_right, mr * sr - mi * si, mr * si + mi * sr)
        factor = 1.0 - measured_all[slot].astype(jnp.float32) * lax.rsqrt(
            dr * dr + di * di + smooth_floor
        )
        br, bi = transform(fourier_right, fourier_left, factor * dr, factor * di)
        add(1, 0, br * mr + bi * mi)
        add(1, 1, bi * mr - br * mi)
        nr, ni = transform(near_right, near_left, br * sr + bi * si, bi * sr - br * si)
        add(0, 0, nr * pr + ni * pi)
        add(0, 1, ni * pr - nr * pi)
        return carry

    lax.fori_loop(0, used[0], one_slot, 0)
    inside[...] = total[:, :, half : half + tile, :full]
    upper_rim[...] = total[:, :, :half, :full].astype(jnp.bfloat16)
    lower_rim[...] = total[:, :, half + tile : full, :full].astype(jnp.bfloat16)


def slots_gradient(corners, used, pieces, probe_wave, measured_all, tables):
    size = probe_wave.shape[1]
    half = size // 2
    tile = pieces[0].shape[2]
    full = tile + 2 * half
    vmem = pl.BlockSpec(memory_space=pltpu.VMEM)
    smem = pl.BlockSpec(memory_space=pltpu.SMEM)
    return pl.pallas_call(
        slots_kernel,
        out_shape=[
            jax.ShapeDtypeStruct((2, 2, tile, full), jnp.float32),
            jax.ShapeDtypeStruct((2, 2, half, full), jnp.bfloat16),
            jax.ShapeDtypeStruct((2, 2, half, full), jnp.bfloat16),
        ],
        in_specs=[smem, smem] + [vmem] * 11,
        out_specs=[vmem] * 3,
        scratch_shapes=[
            pltpu.VMEM((2, 2, full + ROWS, full + LANES), jnp.float32),
            pltpu.VMEM((2, 2, full + ROWS, full + LANES), jnp.float32),
        ],
        compiler_params=pltpu.CompilerParams(vmem_limit_bytes=56 * 2**20),
    )(corners, used, *pieces, probe_wave, measured_all, *tables)


def shards(object_field, probe_wave, positions, counts, amplitudes):
    size = probe_wave.shape[1]
    half = size // 2
    slot_total = positions.shape[2]
    tile = object_field.shape[2]
    tables = make_tables(size)
    corners = positions.reshape(slot_total, 2)
    measured_all = amplitudes.reshape(slot_total, size, size)
    used = counts.reshape(1)
    current = object_field
    for _ in range(ITERS):
        cells = current.astype(jnp.bfloat16)
        left = passed_along(cells[:, :, :, tile - half :], "col", 1)
        right = passed_along(cells[:, :, :, :half], "col", -1)
        band = jnp.concatenate([left, cells, right], axis=3)
        top = passed_along(band[:, :, tile - half :], "row", 1)
        bottom = passed_along(band[:, :, :half], "row", -1)
        inside, upper_rim, lower_rim = slots_gradient(
            corners, used, (current, left, right, top, bottom), probe_wave, measured_all, tables
        )
        from_below = passed_along(upper_rim, "row", -1).astype(jnp.float32)
        from_above = passed_along(lower_rim, "row", 1).astype(jnp.float32)
        inside = inside.at[:, :, :half].add(from_above)
        inside = inside.at[:, :, tile - half :].add(from_below)
        from_right = passed_along(inside[..., :half].astype(jnp.bfloat16), "col", -1)
        from_left = passed_along(inside[..., half + tile :].astype(jnp.bfloat16), "col", 1)
        summed = inside[..., half : half + tile]
        summed = summed.at[..., :half].add(from_left.astype(jnp.float32))
        summed = summed.at[..., tile - half :].add(from_right.astype(jnp.float32))
        current = current - descent_rate * summed
    return current


def solution(mesh):
    in_specs = (
        P(None, None, "row", "col"),
        P(),
        P("row", "col", None, None),
        P("row", "col"),
        P("row", "col", None, None, None),
    )
    out_specs = P(None, None, "row", "col")
    return jax.shard_map(shards, mesh=mesh, in_specs=in_specs, out_specs=out_specs, check_vma=False)
```

```python
import jax
import jax.numpy as jnp
import ml_dtypes
import numpy as np
from jax import lax
from jax.experimental import pallas as pl
from jax.experimental.pallas import tpu as pltpu
from jax.sharding import PartitionSpec as P

ITERS = 2
LANES = 128
ROWS = 8

smooth_floor = 0.25
descent_rate = 0.1


def make_tables(points):
    indices = np.arange(points)
    phases = 2.0 * np.pi / points * (indices[:, None] * indices[None, :] % points)
    fourier = np.exp(-1j * phases) / np.sqrt(points)
    frequency = np.where(indices < points // 2, indices, indices - points).astype(np.float64)
    chirp = np.exp(-1j * np.pi / (2.0 * points) * frequency * frequency)
    kernel = (np.exp(1j * phases) @ chirp) / points
    propagator = kernel[(indices[:, None] - indices[None, :]) % points]
    forms = []
    for matrix in (fourier, propagator):
        real = matrix.real.astype(np.float32).astype(ml_dtypes.bfloat16)
        imag = matrix.imag.astype(np.float32).astype(ml_dtypes.bfloat16)
        forms.append(np.block([[real, -imag], [imag, real]]))
        forms.append(np.block([[real, imag], [-imag, real]]))
    return [jnp.asarray(form) for form in forms]


def transform(left_form, right_form, real, imag):
    size = real.shape[0]
    stacked = jnp.concatenate([real.astype(jnp.bfloat16), imag.astype(jnp.bfloat16)], axis=0)
    inner = jnp.dot(left_form[...], stacked, preferred_element_type=jnp.float32)
    inner = inner.astype(jnp.bfloat16)
    joined = jnp.concatenate([inner[:size], inner[size:]], axis=1)
    outer = jnp.dot(joined, right_form[...], preferred_element_type=jnp.float32)
    return outer[:, :size], outer[:, size:]


def rounded(value):
    return value.astype(jnp.bfloat16).astype(jnp.float32)


def slots_kernel(
    corners, used, core, left, right, top, bottom,
    top_left, top_right, bottom_left, bottom_right, probe, measured_all,
    fourier_left, fourier_right, near_left, near_right,
    inside, upper_rim, lower_rim, frame, total,
):
    size = probe.shape[1]
    half = size // 2
    tile = core.shape[2]
    full = tile + 2 * half
    wide = size + LANES
    tall = size + ROWS
    for part in range(2):
        lift = 1.0 if part == 0 else 0.0
        for layer in range(2):
            at = (layer, part)
            low, mid, high = (0, half), (half, half + tile), (half + tile, full)
            for piece, rows, columns in (
                (core, mid, mid), (left, mid, low), (right, mid, high),
                (top, low, mid), (bottom, high, mid), (top_left, low, low),
                (top_right, low, high), (bottom_left, high, low), (bottom_right, high, high),
            ):
                frame[layer, part, rows[0] : rows[1], columns[0] : columns[1]] = (
                    piece[at].astype(jnp.bfloat16).astype(jnp.float32) + lift
                )
    total[...] = jnp.zeros_like(total)

    def one_slot(slot, carry):
        y = corners[slot, 0]
        x = corners[slot, 1]
        shift = lax.rem(x, LANES)
        base = pl.multiple_of(x - shift, LANES)
        down = lax.rem(y, ROWS)
        start = pl.multiple_of(y - down, ROWS)

        def window(layer, part):
            value = frame[layer, part, pl.ds(start, tall), pl.ds(base, wide)]
            value = pltpu.roll(value, lax.rem(wide - shift, wide), 1)[:, :size]
            return pltpu.roll(value, lax.rem(tall - down, tall), 0)[:size]

        def add(layer, part, value):
            value = jnp.concatenate([value, jnp.zeros((ROWS, size), jnp.float32)], axis=0)
            value = pltpu.roll(value, down, 0)
            value = jnp.concatenate([value, jnp.zeros((tall, LANES), jnp.float32)], axis=1)
            total[layer, part, pl.ds(start, tall), pl.ds(base, wide)] += pltpu.roll(value, shift, 1)

        fr, fi = window(0, 0), window(0, 1)
        pr, pi = probe[0], probe[1]
        mr, mi = transform(near_left, near_right, pr * fr - pi * fi, pr * fi + pi * fr)
        mr, mi = rounded(mr), rounded(mi)
        sr, si = window(1, 0), window(1, 1)
        dr, di = transform(fourier_left, fourier_right, mr * sr - mi * si, mr * si + mi * sr)
        factor = 1.0 - measured_all[slot].astype(jnp.float32) * lax.rsqrt(
            dr * dr + di * di + smooth_floor
        )
        br, bi = transform(fourier_right, fourier_left, factor * dr, factor * di)
        add(1, 0, br * mr + bi * mi)
        add(1, 1, bi * mr - br * mi)
        nr, ni = transform(near_right, near_left, br * sr + bi * si, bi * sr - br * si)
        add(0, 0, nr * pr + ni * pi)
        add(0, 1, ni * pr - nr * pi)
        return carry

    lax.fori_loop(0, used[0], one_slot, 0)
    inside[...] = total[:, :, half : half + tile, :full]
    upper_rim[...] = total[:, :, :half, :full].astype(jnp.bfloat16)
    lower_rim[...] = total[:, :, half + tile : full, :full].astype(jnp.bfloat16)


def slots_gradient(corners, used, pieces, probe_wave, measured_all, tables):
    size = probe_wave.shape[1]
    half = size // 2
    tile = pieces[0].shape[2]
    full = tile + 2 * half
    vmem = pl.BlockSpec(memory_space=pltpu.VMEM)
    smem = pl.BlockSpec(memory_space=pltpu.SMEM)
    return pl.pallas_call(
        slots_kernel,
        out_shape=[
            jax.ShapeDtypeStruct((2, 2, tile, full), jnp.float32),
            jax.ShapeDtypeStruct((2, 2, half, full), jnp.bfloat16),
            jax.ShapeDtypeStruct((2, 2, half, full), jnp.bfloat16),
        ],
        in_specs=[smem, smem] + [vmem] * 15,
        out_specs=[vmem] * 3,
        scratch_shapes=[
            pltpu.VMEM((2, 2, full + ROWS, full + LANES), jnp.float32),
            pltpu.VMEM((2, 2, full + ROWS, full + LANES), jnp.float32),
        ],
        compiler_params=pltpu.CompilerParams(vmem_limit_bytes=56 * 2**20),
    )(corners, used, *pieces, probe_wave, measured_all, *tables)


OPPOSITE = {"up": "down", "down": "up", "left": "right", "right": "left"}


class Links:
    def __init__(self, send_sems, recv_sems):
        row, col = lax.axis_index("row"), lax.axis_index("col")
        self.has = {
            "up": row > 0,
            "down": row < lax.axis_size("row") - 1,
            "left": col > 0,
            "right": col < lax.axis_size("col") - 1,
        }
        self.target = {
            "up": {"row": row - 1, "col": col},
            "down": {"row": row + 1, "col": col},
            "left": {"row": row, "col": col - 1},
            "right": {"row": row, "col": col + 1},
        }
        self.send_sems, self.recv_sems = send_sems, recv_sems
        self.number = 0
        self.pieces = []

    def greet(self):
        barrier = pltpu.get_barrier_semaphore()
        for toward in OPPOSITE:
            @pl.when(self.has[toward])
            def _(toward=toward):
                pl.semaphore_signal(
                    barrier, inc=1, device_id=self.target[toward],
                    device_id_type=pl.DeviceIdType.MESH,
                )
        pl.semaphore_wait(barrier, sum(has.astype(jnp.int32) for has in self.has.values()))

    def start(self, source, landing, toward, side=None):
        copy = pltpu.make_async_remote_copy(
            src_ref=source,
            dst_ref=landing,
            send_sem=self.send_sems.at[self.number],
            recv_sem=self.recv_sems.at[self.number],
            device_id=self.target[toward],
            device_id_type=pl.DeviceIdType.MESH,
        )
        self.number += 1
        sent, got = self.has[toward], self.has[OPPOSITE[toward]]
        if side is not None:
            sent, got = sent & self.has[side], got & self.has[side]

        @pl.when(sent)
        def _():
            copy.start()

        @pl.when(jnp.logical_not(got))
        def _():
            landing[...] = jnp.zeros(landing.shape, landing.dtype)

        self.pieces.append((copy, sent))
        return copy, got

    def arrived(self, *started):
        for copy, got in started:
            @pl.when(got)
            def _(copy=copy):
                copy.wait_recv()

    def finish(self):
        for copy, sent in self.pieces:
            @pl.when(sent)
            def _(copy=copy):
                copy.wait_send()


def send_halo(links, cells, edges, halo):
    left, right, top, bottom, top_left, top_right, bottom_left, bottom_right = halo
    to_left, to_right, to_up, to_down = edges
    half = to_left.shape[3]
    tile = cells.shape[2]
    to_left[...] = cells[:, :, :, :half].astype(jnp.bfloat16)
    one = links.start(to_left, right, "left")
    to_right[...] = cells[:, :, :, tile - half :].astype(jnp.bfloat16)
    two = links.start(to_right, left, "right")
    to_up[...] = cells[:, :, :half].astype(jnp.bfloat16)
    rest = [links.start(to_up, bottom, "up")]
    to_down[...] = cells[:, :, tile - half :].astype(jnp.bfloat16)
    rest.append(links.start(to_down, top, "down"))
    first, last = pl.ds(0, half), pl.ds(tile - half, half)
    links.arrived(two)
    rest.append(links.start(left.at[:, :, first], bottom_left, "up", "left"))
    rest.append(links.start(left.at[:, :, last], top_left, "down", "left"))
    links.arrived(one)
    rest.append(links.start(right.at[:, :, first], bottom_right, "up", "right"))
    rest.append(links.start(right.at[:, :, last], top_right, "down", "right"))
    links.arrived(*rest)


def fold_in(links, current, inside, upper, lower, updated, landings):
    up_l, up_r, down_l, down_r, up_c, down_c, got_l, got_r, col_l, col_r = landings
    tile = current.shape[2]
    half = upper.shape[2]
    left, mid, right = pl.ds(0, half), pl.ds(half, tile), pl.ds(half + tile, half)
    corners = []
    for side, columns, up, down in (("left", left, up_l, down_l), ("right", right, up_r, down_r)):
        corners.append((
            links.start(upper.at[:, :, :, columns], up, "up", side),
            links.start(lower.at[:, :, :, columns], down, "down", side),
        ))
    centre = (
        links.start(upper.at[:, :, :, mid], up_c, "up"),
        links.start(lower.at[:, :, :, mid], down_c, "down"),
    )

    def both(columns, up, down):
        from_above, from_below = down[...].astype(jnp.float32), up[...].astype(jnp.float32)
        gap = [jnp.zeros(inside.shape[:2] + (tile - 2 * half, up.shape[3]), jnp.float32)]
        return inside[:, :, :, columns] + jnp.concatenate(
            [from_above] + gap * (tile > 2 * half) + [from_below], axis=2
        )

    links.arrived(*corners[0])
    col_l[...] = both(left, up_l, down_l).astype(jnp.bfloat16)
    one = links.start(col_l, got_r, "left")
    links.arrived(*corners[1])
    col_r[...] = both(right, up_r, down_r).astype(jnp.bfloat16)
    two = links.start(col_r, got_l, "right")
    links.arrived(*centre)
    updated[...] = current[...] - descent_rate * both(mid, up_c, down_c)
    links.arrived(one, two)
    updated[:, :, :, :half] -= descent_rate * got_l[...].astype(jnp.float32)
    updated[:, :, :, tile - half :] -= descent_rate * got_r[...].astype(jnp.float32)


def halo_kernel(current, *refs):
    halo, edges, sems = refs[:8], refs[8:12], refs[12:]
    links = Links(*sems)
    links.greet()
    send_halo(links, current, edges, halo)
    links.finish()


def turn_kernel(current, inside, upper, lower, updated, *refs):
    halo, edges, landings, sems = refs[:8], refs[8:12], refs[12:22], refs[22:]
    links = Links(*sems)
    links.greet()
    fold_in(links, current, inside, upper, lower, updated, landings)
    send_halo(links, updated, edges, halo)
    links.finish()


def last_kernel(current, inside, upper, lower, updated, *refs):
    links = Links(*refs[10:])
    links.greet()
    fold_in(links, current, inside, upper, lower, updated, refs[:10])
    links.finish()


def exchange(kernel, collective, half, current, gradient=(), with_halo=True):
    tile = current.shape[2]
    kind = jnp.bfloat16
    flat, tall, square = (2, 2, half, tile), (2, 2, tile, half), (2, 2, half, half)
    outs, scratch, copies = [], [], 0
    if gradient:
        outs.append(jax.ShapeDtypeStruct(current.shape, jnp.float32))
    if with_halo:
        shapes = [tall, tall, flat, flat, square, square, square, square]
        outs += [jax.ShapeDtypeStruct(shape, kind) for shape in shapes]
        scratch += [pltpu.VMEM(shape, kind) for shape in (tall, tall, flat, flat)]
        copies += 8
    if gradient:
        shapes = [square] * 4 + [flat] * 2 + [tall] * 4
        scratch += [pltpu.VMEM(shape, kind) for shape in shapes]
        copies += 8
    vmem = pl.BlockSpec(memory_space=pltpu.VMEM)
    return pl.pallas_call(
        kernel,
        out_shape=outs,
        in_specs=[vmem] * (1 + len(gradient)),
        out_specs=[vmem] * len(outs),
        scratch_shapes=scratch + [pltpu.SemaphoreType.DMA((copies,))] * 2,
        compiler_params=pltpu.CompilerParams(
            collective_id=collective, has_side_effects=True, vmem_limit_bytes=40 * 2**20
        ),
    )(current, *gradient)


def shards(object_field, probe_wave, positions, counts, amplitudes):
    size = probe_wave.shape[1]
    half = size // 2
    slot_total = positions.shape[2]
    tables = make_tables(size)
    corners = positions.reshape(slot_total, 2)
    measured_all = amplitudes.reshape(slot_total, size, size)
    used = counts.reshape(1)
    current = object_field
    halo = exchange(halo_kernel, 0, half, current)
    for iteration in range(ITERS):
        gradient = slots_gradient(
            corners, used, (current, *halo), probe_wave, measured_all, tables
        )
        if iteration < ITERS - 1:
            current, *halo = exchange(turn_kernel, 1, half, current, tuple(gradient))
        else:
            (current,) = exchange(last_kernel, 2, half, current, tuple(gradient), False)
    return current


def solution(mesh):
    in_specs = (
        P(None, None, "row", "col"),
        P(),
        P("row", "col", None, None),
        P("row", "col"),
        P("row", "col", None, None, None),
    )
    out_specs = P(None, None, "row", "col")
    return jax.shard_map(shards, mesh=mesh, in_specs=in_specs, out_specs=out_specs, check_vma=False)
```

```python
import jax
import jax.numpy as jnp
import ml_dtypes
import numpy as np
from jax import lax
from jax.experimental import pallas as pl
from jax.experimental.pallas import tpu as pltpu
from jax.sharding import PartitionSpec as P

ITERS = 2
LANES = 128
ROWS = 8

smooth_floor = 0.25
descent_rate = 0.1


def make_tables(points):
    indices = np.arange(points)
    phases = 2.0 * np.pi / points * (indices[:, None] * indices[None, :] % points)
    fourier = np.exp(-1j * phases) / np.sqrt(points)
    frequency = np.where(indices < points // 2, indices, indices - points).astype(np.float64)
    chirp = np.exp(-1j * np.pi / (2.0 * points) * frequency * frequency)
    kernel = (np.exp(1j * phases) @ chirp) / points
    propagator = kernel[(indices[:, None] - indices[None, :]) % points]
    forms = []
    for matrix in (fourier, propagator):
        real = matrix.real.astype(np.float32).astype(ml_dtypes.bfloat16)
        imag = matrix.imag.astype(np.float32).astype(ml_dtypes.bfloat16)
        forms.append(np.block([[real, -imag], [imag, real]]))
        forms.append(np.block([[real, imag], [-imag, real]]))
    return [jnp.asarray(form) for form in forms]


def transform(left_form, right_form, real, imag):
    size = real.shape[0]
    stacked = jnp.concatenate([real.astype(jnp.bfloat16), imag.astype(jnp.bfloat16)], axis=0)
    inner = jnp.dot(left_form[...], stacked, preferred_element_type=jnp.float32)
    inner = inner.astype(jnp.bfloat16)
    joined = jnp.concatenate([inner[:size], inner[size:]], axis=1)
    outer = jnp.dot(joined, right_form[...], preferred_element_type=jnp.float32)
    return outer[:, :size], outer[:, size:]


def rounded(value):
    return value.astype(jnp.bfloat16).astype(jnp.float32)


def slots_kernel(
    corners, used, core, left, right, top, bottom,
    top_left, top_right, bottom_left, bottom_right, probe, measured_all,
    fourier_left, fourier_right, near_left, near_right,
    inside, upper_rim, lower_rim, frame, total,
):
    size = probe.shape[1]
    half = size // 2
    tile = core.shape[2]
    full = tile + 2 * half
    wide = size + LANES
    tall = size + ROWS
    for part in range(2):
        lift = 1.0 if part == 0 else 0.0
        for layer in range(2):
            at = (layer, part)
            low, mid, high = (0, half), (half, half + tile), (half + tile, full)
            for piece, rows, columns in (
                (core, mid, mid), (left, mid, low), (right, mid, high),
                (top, low, mid), (bottom, high, mid), (top_left, low, low),
                (top_right, low, high), (bottom_left, high, low), (bottom_right, high, high),
            ):
                frame[layer, part, rows[0] : rows[1], columns[0] : columns[1]] = (
                    piece[at].astype(jnp.bfloat16).astype(jnp.float32) + lift
                )
    total[...] = jnp.zeros_like(total)

    def slot_grads(slot):
        y = corners[slot, 0]
        x = corners[slot, 1]
        shift = lax.rem(x, LANES)
        base = pl.multiple_of(x - shift, LANES)
        down = lax.rem(y, ROWS)
        start = pl.multiple_of(y - down, ROWS)

        def window(layer, part):
            value = frame[layer, part, pl.ds(start, tall), pl.ds(base, wide)]
            value = pltpu.roll(value, lax.rem(wide - shift, wide), 1)[:, :size]
            return pltpu.roll(value, lax.rem(tall - down, tall), 0)[:size]

        def placed(value):
            value = jnp.concatenate([value, jnp.zeros((ROWS, size), jnp.float32)], axis=0)
            value = pltpu.roll(value, down, 0)
            value = jnp.concatenate([value, jnp.zeros((tall, LANES), jnp.float32)], axis=1)
            return pltpu.roll(value, shift, 1)

        fr, fi = window(0, 0), window(0, 1)
        pr, pi = probe[0], probe[1]
        mr, mi = transform(near_left, near_right, pr * fr - pi * fi, pr * fi + pi * fr)
        yield
        mr, mi = rounded(mr), rounded(mi)
        sr, si = window(1, 0), window(1, 1)
        dr, di = transform(fourier_left, fourier_right, mr * sr - mi * si, mr * si + mi * sr)
        yield
        factor = 1.0 - measured_all[slot].astype(jnp.float32) * lax.rsqrt(
            dr * dr + di * di + smooth_floor
        )
        br, bi = transform(fourier_right, fourier_left, factor * dr, factor * di)
        yield
        nr, ni = transform(near_right, near_left, br * sr + bi * si, bi * sr - br * si)
        yield
        spot = (pl.ds(start, tall), pl.ds(base, wide))
        total[(1, 0) + spot] += placed(br * mr + bi * mi)
        total[(1, 1) + spot] += placed(bi * mr - br * mi)
        total[(0, 0) + spot] += placed(nr * pr + ni * pi)
        total[(0, 1) + spot] += placed(ni * pr - nr * pi)
        yield

    def together(*slots):
        for _ in zip(*[slot_grads(slot) for slot in slots]):
            pass

    def two_slots(pair, carry):
        together(2 * pair, 2 * pair + 1)
        return carry

    pairs = used[0] // 2
    lax.fori_loop(0, pairs, two_slots, 0)

    @pl.when(used[0] > 2 * pairs)
    def _():
        together(used[0] - 1)

    inside[...] = total[:, :, half : half + tile, :full]
    upper_rim[...] = total[:, :, :half, :full].astype(jnp.bfloat16)
    lower_rim[...] = total[:, :, half + tile : full, :full].astype(jnp.bfloat16)


def slots_gradient(corners, used, pieces, probe_wave, measured_all, tables):
    size = probe_wave.shape[1]
    half = size // 2
    tile = pieces[0].shape[2]
    full = tile + 2 * half
    vmem = pl.BlockSpec(memory_space=pltpu.VMEM)
    smem = pl.BlockSpec(memory_space=pltpu.SMEM)
    return pl.pallas_call(
        slots_kernel,
        out_shape=[
            jax.ShapeDtypeStruct((2, 2, tile, full), jnp.float32),
            jax.ShapeDtypeStruct((2, 2, half, full), jnp.bfloat16),
            jax.ShapeDtypeStruct((2, 2, half, full), jnp.bfloat16),
        ],
        in_specs=[smem, smem] + [vmem] * 15,
        out_specs=[vmem] * 3,
        scratch_shapes=[
            pltpu.VMEM((2, 2, full + ROWS, full + LANES), jnp.float32),
            pltpu.VMEM((2, 2, full + ROWS, full + LANES), jnp.float32),
        ],
        compiler_params=pltpu.CompilerParams(vmem_limit_bytes=30 * 2**20),
    )(corners, used, *pieces, probe_wave, measured_all, *tables)


OPPOSITE = {"up": "down", "down": "up", "left": "right", "right": "left"}


class Links:
    def __init__(self, send_sems, recv_sems):
        row, col = lax.axis_index("row"), lax.axis_index("col")
        self.has = {
            "up": row > 0,
            "down": row < lax.axis_size("row") - 1,
            "left": col > 0,
            "right": col < lax.axis_size("col") - 1,
        }
        self.target = {
            "up": {"row": row - 1, "col": col},
            "down": {"row": row + 1, "col": col},
            "left": {"row": row, "col": col - 1},
            "right": {"row": row, "col": col + 1},
        }
        self.send_sems, self.recv_sems = send_sems, recv_sems
        self.number = 0
        self.pieces = []

    def greet(self):
        barrier = pltpu.get_barrier_semaphore()
        for toward in OPPOSITE:
            @pl.when(self.has[toward])
            def _(toward=toward):
                pl.semaphore_signal(
                    barrier, inc=1, device_id=self.target[toward],
                    device_id_type=pl.DeviceIdType.MESH,
                )
        pl.semaphore_wait(barrier, sum(has.astype(jnp.int32) for has in self.has.values()))

    def start(self, source, landing, toward, side=None):
        copy = pltpu.make_async_remote_copy(
            src_ref=source,
            dst_ref=landing,
            send_sem=self.send_sems.at[self.number],
            recv_sem=self.recv_sems.at[self.number],
            device_id=self.target[toward],
            device_id_type=pl.DeviceIdType.MESH,
        )
        self.number += 1
        sent, got = self.has[toward], self.has[OPPOSITE[toward]]
        if side is not None:
            sent, got = sent & self.has[side], got & self.has[side]

        @pl.when(sent)
        def _():
            copy.start()

        @pl.when(jnp.logical_not(got))
        def _():
            landing[...] = jnp.zeros(landing.shape, landing.dtype)

        self.pieces.append((copy, sent))
        return copy, got

    def arrived(self, *started):
        for copy, got in started:
            @pl.when(got)
            def _(copy=copy):
                copy.wait_recv()

    def finish(self):
        for copy, sent in self.pieces:
            @pl.when(sent)
            def _(copy=copy):
                copy.wait_send()


def send_halo(links, cells, edges, halo):
    left, right, top, bottom, top_left, top_right, bottom_left, bottom_right = halo
    to_left, to_right, to_up, to_down = edges
    half = to_left.shape[3]
    tile = cells.shape[2]
    to_left[...] = cells[:, :, :, :half].astype(jnp.bfloat16)
    one = links.start(to_left, right, "left")
    to_right[...] = cells[:, :, :, tile - half :].astype(jnp.bfloat16)
    two = links.start(to_right, left, "right")
    to_up[...] = cells[:, :, :half].astype(jnp.bfloat16)
    rest = [links.start(to_up, bottom, "up")]
    to_down[...] = cells[:, :, tile - half :].astype(jnp.bfloat16)
    rest.append(links.start(to_down, top, "down"))
    first, last = pl.ds(0, half), pl.ds(tile - half, half)
    links.arrived(two)
    rest.append(links.start(left.at[:, :, first], bottom_left, "up", "left"))
    rest.append(links.start(left.at[:, :, last], top_left, "down", "left"))
    links.arrived(one)
    rest.append(links.start(right.at[:, :, first], bottom_right, "up", "right"))
    rest.append(links.start(right.at[:, :, last], top_right, "down", "right"))
    links.arrived(*rest)


def fold_in(links, current, inside, upper, lower, updated, landings):
    up_l, up_r, down_l, down_r, up_c, down_c, got_l, got_r, col_l, col_r = landings
    tile = current.shape[2]
    half = upper.shape[2]
    left, mid, right = pl.ds(0, half), pl.ds(half, tile), pl.ds(half + tile, half)
    corners = []
    for side, columns, up, down in (("left", left, up_l, down_l), ("right", right, up_r, down_r)):
        corners.append((
            links.start(upper.at[:, :, :, columns], up, "up", side),
            links.start(lower.at[:, :, :, columns], down, "down", side),
        ))
    centre = (
        links.start(upper.at[:, :, :, mid], up_c, "up"),
        links.start(lower.at[:, :, :, mid], down_c, "down"),
    )

    def both(columns, up, down):
        from_above, from_below = down[...].astype(jnp.float32), up[...].astype(jnp.float32)
        gap = [jnp.zeros(inside.shape[:2] + (tile - 2 * half, up.shape[3]), jnp.float32)]
        return inside[:, :, :, columns] + jnp.concatenate(
            [from_above] + gap * (tile > 2 * half) + [from_below], axis=2
        )

    links.arrived(*corners[0])
    col_l[...] = both(left, up_l, down_l).astype(jnp.bfloat16)
    one = links.start(col_l, got_r, "left")
    links.arrived(*corners[1])
    col_r[...] = both(right, up_r, down_r).astype(jnp.bfloat16)
    two = links.start(col_r, got_l, "right")
    links.arrived(*centre)
    updated[...] = current[...] - descent_rate * both(mid, up_c, down_c)
    links.arrived(one, two)
    updated[:, :, :, :half] -= descent_rate * got_l[...].astype(jnp.float32)
    updated[:, :, :, tile - half :] -= descent_rate * got_r[...].astype(jnp.float32)


def halo_kernel(current, *refs):
    halo, edges, sems = refs[:8], refs[8:12], refs[12:]
    links = Links(*sems)
    links.greet()
    send_halo(links, current, edges, halo)
    links.finish()


def turn_kernel(current, inside, upper, lower, updated, *refs):
    halo, edges, landings, sems = refs[:8], refs[8:12], refs[12:22], refs[22:]
    links = Links(*sems)
    links.greet()
    fold_in(links, current, inside, upper, lower, updated, landings)
    send_halo(links, updated, edges, halo)
    links.finish()


def last_kernel(current, inside, upper, lower, updated, *refs):
    links = Links(*refs[10:])
    links.greet()
    fold_in(links, current, inside, upper, lower, updated, refs[:10])
    links.finish()


def exchange(kernel, collective, half, current, gradient=(), with_halo=True):
    tile = current.shape[2]
    kind = jnp.bfloat16
    flat, tall, square = (2, 2, half, tile), (2, 2, tile, half), (2, 2, half, half)
    outs, scratch, copies = [], [], 0
    if gradient:
        outs.append(jax.ShapeDtypeStruct(current.shape, jnp.float32))
    if with_halo:
        shapes = [tall, tall, flat, flat, square, square, square, square]
        outs += [jax.ShapeDtypeStruct(shape, kind) for shape in shapes]
        scratch += [pltpu.VMEM(shape, kind) for shape in (tall, tall, flat, flat)]
        copies += 8
    if gradient:
        shapes = [square] * 4 + [flat] * 2 + [tall] * 4
        scratch += [pltpu.VMEM(shape, kind) for shape in shapes]
        copies += 8
    vmem = pl.BlockSpec(memory_space=pltpu.VMEM)
    return pl.pallas_call(
        kernel,
        out_shape=outs,
        in_specs=[vmem] * (1 + len(gradient)),
        out_specs=[vmem] * len(outs),
        scratch_shapes=scratch + [pltpu.SemaphoreType.DMA((copies,))] * 2,
        compiler_params=pltpu.CompilerParams(
            collective_id=collective, has_side_effects=True, vmem_limit_bytes=24 * 2**20
        ),
    )(current, *gradient)


def shards(object_field, probe_wave, positions, counts, amplitudes):
    size = probe_wave.shape[1]
    half = size // 2
    slot_total = positions.shape[2]
    tables = make_tables(size)
    corners = positions.reshape(slot_total, 2)
    measured_all = amplitudes.reshape(slot_total, size, size)
    used = counts.reshape(1)
    current = object_field
    halo = exchange(halo_kernel, 0, half, current)
    for iteration in range(ITERS):
        gradient = slots_gradient(
            corners, used, (current, *halo), probe_wave, measured_all, tables
        )
        if iteration < ITERS - 1:
            current, *halo = exchange(turn_kernel, 1, half, current, tuple(gradient))
        else:
            (current,) = exchange(last_kernel, 2, half, current, tuple(gradient), False)
    return current


def solution(mesh):
    in_specs = (
        P(None, None, "row", "col"),
        P(),
        P("row", "col", None, None),
        P("row", "col"),
        P("row", "col", None, None, None),
    )
    out_specs = P(None, None, "row", "col")
    return jax.shard_map(shards, mesh=mesh, in_specs=in_specs, out_specs=out_specs, check_vma=False)
```

```python
import jax
import jax.numpy as jnp
import ml_dtypes
import numpy as np
from jax import lax
from jax.experimental import pallas as pl
from jax.experimental.pallas import tpu as pltpu
from jax.sharding import PartitionSpec as P

ITERS = 2
LANES = 128
ROWS = 8

smooth_floor = 0.25
descent_rate = 0.1


def make_tables(points):
    indices = np.arange(points)
    phases = 2.0 * np.pi / points * (indices[:, None] * indices[None, :] % points)
    fourier = np.exp(-1j * phases) / np.sqrt(points)
    frequency = np.where(indices < points // 2, indices, indices - points).astype(np.float64)
    chirp = np.exp(-1j * np.pi / (2.0 * points) * frequency * frequency)
    kernel = (np.exp(1j * phases) @ chirp) / points
    propagator = kernel[(indices[:, None] - indices[None, :]) % points]
    forms = []
    for matrix in (fourier, propagator):
        real = matrix.real.astype(np.float32).astype(ml_dtypes.bfloat16)
        imag = matrix.imag.astype(np.float32).astype(ml_dtypes.bfloat16)
        forms.append(np.block([[real, -imag], [imag, real]]))
        forms.append(np.block([[real, imag], [-imag, real]]))
    return jnp.asarray(np.stack(forms))


def transform(left_form, right_form, real, imag):
    size = real.shape[0]
    stacked = jnp.concatenate([real.astype(jnp.bfloat16), imag.astype(jnp.bfloat16)], axis=0)
    inner = jnp.dot(left_form[...], stacked, preferred_element_type=jnp.float32)
    inner = inner.astype(jnp.bfloat16)
    joined = jnp.concatenate([inner[:size], inner[size:]], axis=1)
    outer = jnp.dot(joined, right_form[...], preferred_element_type=jnp.float32)
    return outer[:, :size], outer[:, size:]


def rounded(value):
    return value.astype(jnp.bfloat16).astype(jnp.float32)


def slots_kernel(
    corners, used, core, left, right, top, bottom,
    top_left, top_right, bottom_left, bottom_right, probe, measured_all,
    tables, inside, upper_rim, lower_rim, frame, total,
):
    fourier_left, fourier_right, near_left, near_right = [tables.at[form] for form in range(4)]
    size = probe.shape[1]
    half = size // 2
    tile = core.shape[2]
    full = tile + 2 * half
    wide = size + LANES
    tall = size + ROWS
    for part in range(2):
        lift = 1.0 if part == 0 else 0.0
        for layer in range(2):
            at = (layer, part)
            low, mid, high = (0, half), (half, half + tile), (half + tile, full)
            for piece, rows, columns in (
                (core, mid, mid), (left, mid, low), (right, mid, high),
                (top, low, mid), (bottom, high, mid), (top_left, low, low),
                (top_right, low, high), (bottom_left, high, low), (bottom_right, high, high),
            ):
                frame[layer, part, rows[0] : rows[1], columns[0] : columns[1]] = (
                    piece[at].astype(jnp.bfloat16).astype(jnp.float32) + lift
                )
    total[...] = jnp.zeros_like(total)

    def slot_grads(slot):
        y = corners[slot, 0]
        x = corners[slot, 1]
        shift = lax.rem(x, LANES)
        base = pl.multiple_of(x - shift, LANES)
        down = lax.rem(y, ROWS)
        start = pl.multiple_of(y - down, ROWS)

        def window(layer, part):
            value = frame[layer, part, pl.ds(start, tall), pl.ds(base, wide)]
            value = pltpu.roll(value, lax.rem(wide - shift, wide), 1)[:, :size]
            return pltpu.roll(value, lax.rem(tall - down, tall), 0)[:size]

        def placed(value):
            value = jnp.concatenate([value, jnp.zeros((ROWS, size), jnp.float32)], axis=0)
            value = pltpu.roll(value, down, 0)
            value = jnp.concatenate([value, jnp.zeros((tall, LANES), jnp.float32)], axis=1)
            return pltpu.roll(value, shift, 1)

        fr, fi = window(0, 0), window(0, 1)
        pr, pi = probe[0], probe[1]
        mr, mi = transform(near_left, near_right, pr * fr - pi * fi, pr * fi + pi * fr)
        yield
        mr, mi = rounded(mr), rounded(mi)
        sr, si = window(1, 0), window(1, 1)
        dr, di = transform(fourier_left, fourier_right, mr * sr - mi * si, mr * si + mi * sr)
        yield
        factor = 1.0 - measured_all[slot].astype(jnp.float32) * lax.rsqrt(
            dr * dr + di * di + smooth_floor
        )
        br, bi = transform(fourier_right, fourier_left, factor * dr, factor * di)
        yield
        nr, ni = transform(near_right, near_left, br * sr + bi * si, bi * sr - br * si)
        yield
        spot = (pl.ds(start, tall), pl.ds(base, wide))
        total[(1, 0) + spot] += placed(br * mr + bi * mi)
        total[(1, 1) + spot] += placed(bi * mr - br * mi)
        total[(0, 0) + spot] += placed(nr * pr + ni * pi)
        total[(0, 1) + spot] += placed(ni * pr - nr * pi)
        yield

    def together(*slots):
        for _ in zip(*[slot_grads(slot) for slot in slots]):
            pass

    def two_slots(pair, carry):
        together(2 * pair, 2 * pair + 1)
        return carry

    pairs = used[0] // 2
    lax.fori_loop(0, pairs, two_slots, 0)

    @pl.when(used[0] > 2 * pairs)
    def _():
        together(used[0] - 1)

    inside[...] = total[:, :, half : half + tile, :full]
    upper_rim[...] = total[:, :, :half, :full].astype(jnp.bfloat16)
    lower_rim[...] = total[:, :, half + tile : full, :full].astype(jnp.bfloat16)


def slots_gradient(corners, used, pieces, probe_wave, measured_all, tables):
    size = probe_wave.shape[1]
    half = size // 2
    tile = pieces[0].shape[2]
    full = tile + 2 * half
    vmem = pl.BlockSpec(memory_space=pltpu.VMEM)
    smem = pl.BlockSpec(memory_space=pltpu.SMEM)
    return pl.pallas_call(
        slots_kernel,
        out_shape=[
            jax.ShapeDtypeStruct((2, 2, tile, full), jnp.float32),
            jax.ShapeDtypeStruct((2, 2, half, full), jnp.bfloat16),
            jax.ShapeDtypeStruct((2, 2, half, full), jnp.bfloat16),
        ],
        in_specs=[smem, smem] + [vmem] * 12,
        out_specs=[vmem] * 3,
        scratch_shapes=[
            pltpu.VMEM((2, 2, full + ROWS, full + LANES), jnp.float32),
            pltpu.VMEM((2, 2, full + ROWS, full + LANES), jnp.float32),
        ],
        compiler_params=pltpu.CompilerParams(vmem_limit_bytes=30 * 2**20),
    )(corners, used, *pieces, probe_wave, measured_all, tables)


OPPOSITE = {"up": "down", "down": "up", "left": "right", "right": "left"}


class Links:
    def __init__(self, send_sems, recv_sems):
        row, col = lax.axis_index("row"), lax.axis_index("col")
        self.has = {
            "up": row > 0,
            "down": row < lax.axis_size("row") - 1,
            "left": col > 0,
            "right": col < lax.axis_size("col") - 1,
        }
        self.target = {
            "up": {"row": row - 1, "col": col},
            "down": {"row": row + 1, "col": col},
            "left": {"row": row, "col": col - 1},
            "right": {"row": row, "col": col + 1},
        }
        self.send_sems, self.recv_sems = send_sems, recv_sems
        self.number = 0
        self.pieces = []

    def greet(self):
        barrier = pltpu.get_barrier_semaphore()
        for toward in OPPOSITE:
            @pl.when(self.has[toward])
            def _(toward=toward):
                pl.semaphore_signal(
                    barrier, inc=1, device_id=self.target[toward],
                    device_id_type=pl.DeviceIdType.MESH,
                )
        pl.semaphore_wait(barrier, sum(has.astype(jnp.int32) for has in self.has.values()))

    def start(self, source, landing, toward, side=None):
        copy = pltpu.make_async_remote_copy(
            src_ref=source,
            dst_ref=landing,
            send_sem=self.send_sems.at[self.number],
            recv_sem=self.recv_sems.at[self.number],
            device_id=self.target[toward],
            device_id_type=pl.DeviceIdType.MESH,
        )
        self.number += 1
        sent, got = self.has[toward], self.has[OPPOSITE[toward]]
        if side is not None:
            sent, got = sent & self.has[side], got & self.has[side]

        @pl.when(sent)
        def _():
            copy.start()

        @pl.when(jnp.logical_not(got))
        def _():
            landing[...] = jnp.zeros(landing.shape, landing.dtype)

        self.pieces.append((copy, sent))
        return copy, got

    def arrived(self, *started):
        for copy, got in started:
            @pl.when(got)
            def _(copy=copy):
                copy.wait_recv()

    def finish(self):
        for copy, sent in self.pieces:
            @pl.when(sent)
            def _(copy=copy):
                copy.wait_send()


def send_halo(links, cells, edges, halo):
    left, right, top, bottom, top_left, top_right, bottom_left, bottom_right = halo
    to_left, to_right, to_up, to_down = edges
    half = to_left.shape[3]
    tile = cells.shape[2]
    to_left[...] = cells[:, :, :, :half].astype(jnp.bfloat16)
    one = links.start(to_left, right, "left")
    to_right[...] = cells[:, :, :, tile - half :].astype(jnp.bfloat16)
    two = links.start(to_right, left, "right")
    to_up[...] = cells[:, :, :half].astype(jnp.bfloat16)
    rest = [links.start(to_up, bottom, "up")]
    to_down[...] = cells[:, :, tile - half :].astype(jnp.bfloat16)
    rest.append(links.start(to_down, top, "down"))
    first, last = pl.ds(0, half), pl.ds(tile - half, half)
    links.arrived(two)
    rest.append(links.start(left.at[:, :, first], bottom_left, "up", "left"))
    rest.append(links.start(left.at[:, :, last], top_left, "down", "left"))
    links.arrived(one)
    rest.append(links.start(right.at[:, :, first], bottom_right, "up", "right"))
    rest.append(links.start(right.at[:, :, last], top_right, "down", "right"))
    links.arrived(*rest)


def fold_in(links, current, inside, upper, lower, updated, landings):
    up_l, up_r, down_l, down_r, up_c, down_c, got_l, got_r, col_l, col_r = landings
    tile = current.shape[2]
    half = upper.shape[2]
    left, mid, right = pl.ds(0, half), pl.ds(half, tile), pl.ds(half + tile, half)
    corners = []
    for side, columns, up, down in (("left", left, up_l, down_l), ("right", right, up_r, down_r)):
        corners.append((
            links.start(upper.at[:, :, :, columns], up, "up", side),
            links.start(lower.at[:, :, :, columns], down, "down", side),
        ))
    centre = (
        links.start(upper.at[:, :, :, mid], up_c, "up"),
        links.start(lower.at[:, :, :, mid], down_c, "down"),
    )

    def both(columns, up, down):
        from_above, from_below = down[...].astype(jnp.float32), up[...].astype(jnp.float32)
        gap = [jnp.zeros(inside.shape[:2] + (tile - 2 * half, up.shape[3]), jnp.float32)]
        return inside[:, :, :, columns] + jnp.concatenate(
            [from_above] + gap * (tile > 2 * half) + [from_below], axis=2
        )

    links.arrived(*corners[0])
    col_l[...] = both(left, up_l, down_l).astype(jnp.bfloat16)
    one = links.start(col_l, got_r, "left")
    links.arrived(*corners[1])
    col_r[...] = both(right, up_r, down_r).astype(jnp.bfloat16)
    two = links.start(col_r, got_l, "right")
    links.arrived(*centre)
    updated[...] = current[...] - descent_rate * both(mid, up_c, down_c)
    links.arrived(one, two)
    updated[:, :, :, :half] -= descent_rate * got_l[...].astype(jnp.float32)
    updated[:, :, :, tile - half :] -= descent_rate * got_r[...].astype(jnp.float32)


def halo_kernel(current, *refs):
    halo, edges, sems = refs[:8], refs[8:12], refs[12:]
    links = Links(*sems)
    links.greet()
    send_halo(links, current, edges, halo)
    links.finish()


def turn_kernel(current, inside, upper, lower, updated, *refs):
    halo, edges, landings, sems = refs[:8], refs[8:12], refs[12:22], refs[22:]
    links = Links(*sems)
    links.greet()
    fold_in(links, current, inside, upper, lower, updated, landings)
    send_halo(links, updated, edges, halo)
    links.finish()


def last_kernel(current, inside, upper, lower, updated, *refs):
    links = Links(*refs[10:])
    links.greet()
    fold_in(links, current, inside, upper, lower, updated, refs[:10])
    links.finish()


def exchange(kernel, collective, half, current, gradient=(), with_halo=True):
    tile = current.shape[2]
    kind = jnp.bfloat16
    flat, tall, square = (2, 2, half, tile), (2, 2, tile, half), (2, 2, half, half)
    outs, scratch, copies = [], [], 0
    if gradient:
        outs.append(jax.ShapeDtypeStruct(current.shape, jnp.float32))
    if with_halo:
        shapes = [tall, tall, flat, flat, square, square, square, square]
        outs += [jax.ShapeDtypeStruct(shape, kind) for shape in shapes]
        scratch += [pltpu.VMEM(shape, kind) for shape in (tall, tall, flat, flat)]
        copies += 8
    if gradient:
        shapes = [square] * 4 + [flat] * 2 + [tall] * 4
        scratch += [pltpu.VMEM(shape, kind) for shape in shapes]
        copies += 8
    vmem = pl.BlockSpec(memory_space=pltpu.VMEM)
    return pl.pallas_call(
        kernel,
        out_shape=outs,
        in_specs=[vmem] * (1 + len(gradient)),
        out_specs=[vmem] * len(outs),
        scratch_shapes=scratch + [pltpu.SemaphoreType.DMA((copies,))] * 2,
        compiler_params=pltpu.CompilerParams(
            collective_id=collective, has_side_effects=True, vmem_limit_bytes=24 * 2**20
        ),
    )(current, *gradient)


def shards(object_field, probe_wave, positions, counts, amplitudes):
    size = probe_wave.shape[1]
    half = size // 2
    slot_total = positions.shape[2]
    tables = make_tables(size)
    corners = positions.reshape(slot_total, 2)
    measured_all = amplitudes.reshape(slot_total, size, size)
    used = counts.reshape(1)
    current = object_field
    halo = exchange(halo_kernel, 0, half, current)
    for iteration in range(ITERS):
        gradient = slots_gradient(
            corners, used, (current, *halo), probe_wave, measured_all, tables
        )
        if iteration < ITERS - 1:
            current, *halo = exchange(turn_kernel, 1, half, current, tuple(gradient))
        else:
            (current,) = exchange(last_kernel, 2, half, current, tuple(gradient), False)
    return current


def solution(mesh):
    in_specs = (
        P(None, None, "row", "col"),
        P(),
        P("row", "col", None, None),
        P("row", "col"),
        P("row", "col", None, None, None),
    )
    out_specs = P(None, None, "row", "col")
    return jax.shard_map(shards, mesh=mesh, in_specs=in_specs, out_specs=out_specs, check_vma=False)
```
